32 devices in a mesh: dp: 4 (over y, x), seq: 8 (over z, core).
Axes of the slice: x: 2, y: 2, z: 4, core: 2. Of those that a mesh axis runs over, the one named last changes fastest.
Arguments:
- q_arrive: bfloat16 [4, 1024, 2048], P('dp', 'seq'), may hold values from -6 to 6
- k_arrive: bfloat16 [4, 1024, 2048], P('dp', 'seq'), may hold values from -6 to 6
- v_arrive: bfloat16 [4, 1024, 2048], P('dp', 'seq'), may hold values from -6 to 6
- source_rank: int32 [4, 256], P(None, 'seq'), may hold values from 0 to 3, as said below
- first_length: int32 [4], replicated, may hold values from 1 to 1023
- filter_taps: bfloat16 [1024, 2048], P('seq'), may hold values from -2 to 2
Outputs:
- operator_out: bfloat16 [4, 1024, 2048], P('dp', 'seq')
The draws below stay inside these ranges and needn't reach their ends.
Inputs may be any that keep to these rules, and one draw needn't show every extreme that they name: For each block position b, source_rank[:, b] is a permutation of the 4 data indices. Of the 32 blocks of one device along seq, at most 16 of one pack come from one source index, and some pair reaches 16.
All inputs are finite; a program needn't handle non-finite values.
Results may differ from the reference program's by a relative error of at most 0.005.
Values may be sent and summed in bfloat16 or wider, within the bound.
A program may use at most 64 MiB of HBM per device.

```python
import math
import jax
import jax.numpy as jnp
from jax import lax

C = 2048
TOK_DEV = 128
BLK = 4
SEQ = 1024
PACKS = 4
BPD = 32
CAP = 16


def draw_source_rank(key, part):
    key = jax.random.fold_in(key, 11)
    ranges = SEQ // TOK_DEV

    def per_range(range_key):
        keys_here = jax.random.split(range_key, 5)
        outer_perm = jax.random.permutation(keys_here[0], PACKS)
        inner_perm = jax.random.permutation(keys_here[1], PACKS)
        common = jax.random.randint(keys_here[2], (), 0, PACKS)
        others = jnp.arange((PACKS - 1) * CAP, dtype=jnp.int32)
        others = (common + 1 + others % (PACKS - 1)) % PACKS
        others = jax.random.permutation(keys_here[3], others)[:BPD - CAP]
        shifts = jnp.concatenate([jnp.full((CAP,), common, jnp.int32), others.astype(jnp.int32)])
        shifts = jax.random.permutation(keys_here[4], shifts)
        return outer_perm[(inner_perm[:, None] + shifts[None, :]) % PACKS].astype(jnp.int32)
    tables = jax.vmap(per_range)(jax.random.split(key, ranges))
    return jnp.transpose(tables, (1, 0, 2)).reshape(PACKS, ranges * BPD)


def envelope(decay, steps):
    scale = jnp.sqrt(2.0 / (decay * (1.0 - jnp.exp(-2.0 * SEQ / decay))))
    return scale[None, :] * jnp.exp(-steps / decay[None, :])


def draw_filter_taps(key, part):
    key = jax.random.fold_in(key, 23)
    keys_here = jax.random.split(key, 4)
    steps = jnp.arange(SEQ, dtype=jnp.float32)[:, None]
    short_decay = jnp.exp(jax.random.uniform(keys_here[0], (C,), jnp.float32, math.log(16.0), math.log(120.0)))
    long_decay = jnp.exp(jax.random.uniform(keys_here[1], (C,), jnp.float32, math.log(SEQ / 4.0), math.log(4.0 * SEQ)))
    short_rough = jnp.clip(jax.random.normal(keys_here[2], (SEQ, C), jnp.float32), -4.0, 4.0)
    long_rough = jnp.clip(jax.random.normal(keys_here[3], (SEQ, C), jnp.float32), -4.0, 4.0)
    long_weight = 0.6
    taps = short_rough * envelope(short_decay, steps) + long_weight * long_rough * envelope(long_decay, steps)
    return taps.astype(jnp.bfloat16)


def with_ends(array, key, low, largest):
    spot = [jax.random.randint(jax.random.fold_in(key, axis), (), 0, length) for axis, length in enumerate(array.shape)]
    longest = array.shape.index(max(array.shape))
    next_to = spot[:longest] + [(spot[longest] + 1) % array.shape[longest]] + spot[longest + 1:]
    return array.at[tuple(spot)].set(low).at[tuple(next_to)].set(largest)


def level_of(rng, dims, cuts, low, top_value):
    level, own = 1.0, jax.random.fold_in(rng, 6)
    for position, parts in cuts:
        steps = jnp.exp(jax.random.uniform(jax.random.fold_in(own, position), (parts,), jnp.float32, low / len(cuts), top_value / len(cuts)))
        level = level * jnp.repeat(steps, dims[position] // parts).reshape([-1 if axis == position else 1 for axis in range(len(dims))])
    return level


def noise(stream_key, dims, width, reach, pieces=(), kind=jnp.bfloat16):
    values = jax.random.normal(stream_key, dims, jnp.float32) * width
    if len(pieces) > 0:
        values = level_of(stream_key, dims, pieces, -0.22, 0.18) * values
    return jnp.clip(values, min=-reach, max=reach).astype(kind)


def setup_inputs(seed: int = 0) -> dict:
    key_of = jax.random.split(jax.random.key(seed), 7)
    q_arrive = noise(key_of[0], (PACKS, SEQ, C), 1.0, 6.0, ((0, 4), (1, 8)))
    k_arrive = noise(key_of[1], (PACKS, SEQ, C), 1.0, 6.0, ((0, 4), (1, 8)))
    v_arrive = noise(key_of[2], (PACKS, SEQ, C), 1.0, 6.0, ((0, 4), (1, 8)))
    source_rank = draw_source_rank(jax.random.fold_in(key_of[6], 71), 0)
    first_length = with_ends(jax.random.randint(key_of[4], (PACKS,), 1, SEQ), jax.random.fold_in(key_of[4], 1), 1, SEQ - 1).astype(jnp.int32)
    filter_taps = draw_filter_taps(jax.random.fold_in(key_of[6], 71), 0)
    return {"q_arrive": q_arrive, "k_arrive": k_arrive, "v_arrive": v_arrive, "source_rank": source_rank, "first_length": first_length, "filter_taps": filter_taps}


def reference(q_arrive, k_arrive, v_arrive, source_rank, first_length, filter_taps):
    source_tokens = jnp.repeat(source_rank, BLK, axis=1)
    position_ids = jnp.arange(SEQ, dtype=jnp.int32)[None, :]
    query_pack = q_arrive[source_tokens, position_ids]
    key_pack = k_arrive[source_tokens, position_ids]
    value_pack = v_arrive[source_tokens, position_ids]
    product = (key_pack.astype(jnp.float32) * value_pack.astype(jnp.float32)).astype(jnp.bfloat16)
    later_mask = position_ids >= first_length[:, None]
    later_part = jnp.where(later_mask[:, :, None], product, jnp.zeros_like(product))
    spectrum = jnp.fft.rfft(filter_taps.astype(jnp.float32), n=2 * SEQ, axis=0)

    def per_pack(items):
        whole, later, flags = items

        def convolve(signal):
            grown = jnp.fft.rfft(signal.astype(jnp.float32), n=2 * SEQ, axis=0) * spectrum
            return jnp.fft.irfft(grown, n=2 * SEQ, axis=0)[:SEQ]

        return jnp.where(flags[:, None], convolve(later), convolve(whole)).astype(jnp.float32)

    response = lax.map(per_pack, (product, later_part, later_mask))
    return (query_pack.astype(jnp.float32) * response).astype(jnp.bfloat16)
```

```python
import functools
import math

import jax
import jax.numpy as jnp
import ml_dtypes
import numpy as np
from jax import lax
from jax.experimental import pallas as pl
from jax.experimental.pallas import tpu as pltpu
from jax.sharding import PartitionSpec as P

LANES = 128
FFT_BLOCK = 256
MESH = pl.DeviceIdType.MESH
F32 = jnp.float32
BF16 = jnp.bfloat16


def split_table(table):
    high = table.astype(ml_dtypes.bfloat16)
    low = (table - high.astype(np.float64)).astype(ml_dtypes.bfloat16)
    return high, low


def fourier_tables():
    size = FFT_BLOCK
    freq = np.arange(size)[:, None] * 2 + 1
    angle = math.pi / (2 * size) * (freq * np.arange(size)[None, :] % (4 * size))
    forward = np.concatenate([np.cos(angle), -np.sin(angle)], axis=0)
    places = np.arange(size, 2 * size)[:, None]
    back_angle = math.pi / (2 * size) * (places * freq[:, 0][None, :] % (4 * size))
    inverse = np.concatenate([np.cos(back_angle), -np.sin(back_angle)], axis=1) / size
    return split_table(forward) + split_table(inverse)


def kernel(
    groups, shards, halves, rows, block_len,
    rank_ref, first_ref, q_ref, k_ref, v_ref, f_ref, fwd_hi, fwd_lo, inv_hi, inv_lo,
    out_ref,
    packed, recv, xsend, xbuf, fbuf, rsend, rbuf, xs, spec, fspec, yhi, ylo,
    dp_send, dp_recv, z_send, z_recv,
):
    tokens = q_ref.shape[0]
    blocks = shards * tokens // FFT_BLOCK
    width = halves * LANES
    me_dp = lax.axis_index("dp")
    me_seq = lax.axis_index("seq")
    boundary = first_ref[me_dp]

    barrier = pltpu.get_barrier_semaphore()
    for j in range(1, groups):
        pl.semaphore_signal(
            barrier, inc=1, device_id={"dp": lax.rem(me_dp + j, groups)}, device_id_type=MESH
        )
    for j in range(1, shards):
        pl.semaphore_signal(
            barrier, inc=1, device_id={"seq": lax.rem(me_seq + j, shards)}, device_id_type=MESH
        )

    def lane_tile(index):
        return pl.ds(pl.multiple_of(index * LANES, LANES), LANES)

    def dp_copy(kind, half, j):
        peer = lax.rem(me_dp + j, groups)
        return pltpu.make_async_remote_copy(
            src_ref=packed.at[kind, half, pl.ds(pl.multiple_of(peer * rows, rows), rows)],
            dst_ref=recv.at[kind, half, pl.ds(pl.multiple_of(me_dp * rows, rows), rows)],
            send_sem=dp_send.at[kind, half, j],
            recv_sem=dp_recv.at[kind, half, j],
            device_id={"dp": peer},
            device_id_type=MESH,
        )

    def my_rows():
        return pl.ds(pl.multiple_of(me_seq * tokens, tokens), tokens)

    def z_copy(kind, half, j):
        peer = lax.rem(me_seq + j, shards)
        if kind == 0:
            src = f_ref.at[:, lane_tile(peer * halves + half)]
            dst = fbuf.at[half, my_rows()]
        elif kind == 1:
            src = xsend.at[half, :, lane_tile(peer)]
            dst = xbuf.at[half, my_rows()]
        else:
            src = rsend.at[half, pl.ds(pl.multiple_of(peer * tokens, tokens), tokens)]
            dst = rbuf.at[half, :, lane_tile(me_seq)]
        return pltpu.make_async_remote_copy(
            src_ref=src,
            dst_ref=dst,
            send_sem=z_send.at[kind, half, j],
            recv_sem=z_recv.at[kind, half, j],
            device_id={"seq": peer},
            device_id_type=MESH,
        )

    ranks = rank_ref[...]
    own_rank = rank_ref[pl.ds(me_dp, 1), :]
    own_rank = jnp.broadcast_to(own_rank, ranks.shape)
    group_ids = lax.broadcasted_iota(jnp.int32, ranks.shape, 0)
    earlier_row = lax.broadcasted_iota(jnp.int32, (tokens, tokens), 0)
    earlier_col = lax.broadcasted_iota(jnp.int32, (tokens, tokens), 1)
    earlier = jnp.where(
        (earlier_row // block_len < earlier_col // block_len) & (earlier_row % block_len == 0), 1.0, 0.0
    ).astype(BF16)
    inner = (lax.broadcasted_iota(jnp.int32, ranks.shape, 1) % block_len).astype(F32)
    row_ids = lax.broadcasted_iota(jnp.int32, (rows, tokens), 0).astype(F32)

    def one_hot(mask):
        flags = jnp.where(mask, 1.0, 0.0)
        slots = jnp.dot(flags.astype(BF16), earlier, preferred_element_type=F32)
        target = jnp.where(mask, slots * block_len + inner, -1.0)
        return jnp.concatenate(
            [jnp.where(row_ids == target[p : p + 1], 1.0, 0.0) for p in range(groups)], axis=0
        )

    send_pick = one_hot(ranks == me_dp).astype(BF16)
    recv_pick = jnp.transpose(one_hot(own_rank == group_ids)).astype(BF16)

    def pack(kind, values, tile):
        moved = jnp.dot(send_pick, values, preferred_element_type=F32).astype(BF16)
        for half in range(halves):
            packed[kind, half, :, lane_tile(tile)] = moved[:, half * LANES : (half + 1) * LANES]

    def columns(tile):
        return pl.ds(pl.multiple_of(tile * width, width), width)

    @pl.loop(0, shards)
    def _(tile):
        product = k_ref[:, columns(tile)].astype(F32) * v_ref[:, columns(tile)].astype(F32)
        pack(0, product.astype(BF16), tile)

    pl.semaphore_wait(barrier, groups + shards - 2)
    for half in range(halves):
        for j in range(1, groups):
            dp_copy(0, half, j).start()
    for half in range(halves):
        for j in range(1, shards):
            z_copy(0, half, j).start()

    @pl.loop(0, shards)
    def _(tile):
        pack(1, q_ref[:, columns(tile)], tile)

    for half in range(halves):
        for j in range(1, groups):
            dp_copy(1, half, j).start()
    own = pl.ds(pl.multiple_of(me_dp * rows, rows), rows)
    for half in range(halves):
        for kind in range(2):
            recv[kind, half, own, :] = packed[kind, half, own, :]
        fbuf[half, my_rows(), :] = f_ref[:, lane_tile(me_seq * halves + half)]

    for half in range(halves):
        for j in range(1, groups):
            dp_copy(0, half, j).wait_recv()
        xsend[half] = jnp.dot(recv_pick, recv[0, half], preferred_element_type=F32).astype(BF16)
        for j in range(1, shards):
            z_copy(1, half, j).start()
        xbuf[half, my_rows(), :] = xsend[half, :, lane_tile(me_seq)]

    def forward(values):
        return jnp.dot(fwd_hi[...], values, preferred_element_type=F32) + jnp.dot(
            fwd_lo[...], values, preferred_element_type=F32
        )

    for half in range(halves):
        for j in range(1, shards):
            z_copy(0, half, j).wait_recv()
        for b in range(blocks):
            fspec[half, :, b * LANES : (b + 1) * LANES] = forward(
                fbuf[half, b * FFT_BLOCK : (b + 1) * FFT_BLOCK, :]
            )

    def holds(condition):
        return jnp.where(condition, 1.0, 0.0).astype(F32)

    at_or_after = [holds(FFT_BLOCK * (i + 1) > boundary) for i in range(blocks)]
    before = [1.0 - flag for flag in at_or_after]
    at_block = [
        holds((FFT_BLOCK * i <= boundary) & (FFT_BLOCK * (i + 1) > boundary)) for i in range(blocks)
    ]
    keep = {
        (i, m): jnp.maximum(at_or_after[i], before[m]) for m in range(blocks) for i in range(m)
    }
    place = lax.broadcasted_iota(jnp.int32, (FFT_BLOCK, LANES), 0)
    split = [
        (place + FFT_BLOCK * i < boundary) & (jnp.full(place.shape, FFT_BLOCK * (i + 1)) > boundary)
        for i in range(blocks)
    ]
    extra = blocks * LANES
    step = 16
    sign = jnp.where(lax.broadcasted_iota(jnp.int32, (step, LANES), 0) % 2 == 0, 1.0, -1.0).astype(F32)

    for half in range(halves):
        for j in range(1, shards):
            z_copy(1, half, j).wait_recv()
        early = jnp.zeros((FFT_BLOCK, LANES), F32)
        for i in range(blocks):
            values = xbuf[half, i * FFT_BLOCK : (i + 1) * FFT_BLOCK, :].astype(F32)
            xs[:, i * LANES : (i + 1) * LANES] = jnp.where(split[i], 0.0, values).astype(BF16)
            early = early + jnp.where(split[i] & (place + FFT_BLOCK * i >= 0), values, 0.0) * at_block[i]
        xs[:, extra : extra + LANES] = early.astype(BF16)
        for start in range(0, (blocks + 1) * LANES, 2 * LANES):
            stop = min(start + 2 * LANES, (blocks + 1) * LANES)
            spec[:, start:stop] = forward(xs[:, start:stop])

        @pl.loop(0, FFT_BLOCK // step)
        def _(chunk):
            re = pl.ds(pl.multiple_of(chunk * step, step), step)
            im = pl.ds(pl.multiple_of(FFT_BLOCK + chunk * step, step), step)

            def read(ref, b):
                return ref[re, b * LANES : (b + 1) * LANES], ref[im, b * LANES : (b + 1) * LANES]

            x = [read(spec, b) for b in range(blocks + 1)]
            taps = []
            last = None
            for b in range(blocks):
                a_re, a_im = read(fspec.at[half], b)
                g_re, g_im = sign * a_im, -(sign * a_re)
                if last is not None:
                    g_re, g_im = g_re + last[0], g_im + last[1]
                taps.append((g_re, g_im))
                last = (a_re, a_im)

            def times(a, b):
                return a[0] * b[0] - a[1] * b[1], a[0] * b[1] + a[1] * b[0]

            def put(b, value):
                for part, where in zip(value, (re, im)):
                    high = part.astype(BF16)
                    yhi[where, b * LANES : (b + 1) * LANES] = high
                    ylo[where, b * LANES : (b + 1) * LANES] = (part - high.astype(F32)).astype(BF16)

            edge = times(taps[0], x[blocks])
            for m in range(blocks):
                total = times(taps[0], x[m])
                for i in range(m):
                    term = times(taps[m - i], x[i])
                    total = tuple(t + keep[i, m] * s for t, s in zip(total, term))
                    edge = tuple(t + at_block[m] * s for t, s in zip(edge, term))
                put(m, total)
            put(blocks, edge)

        def inverse(cols):
            return (
                jnp.dot(inv_hi[...], yhi[:, cols], preferred_element_type=F32)
                + jnp.dot(inv_lo[...], yhi[:, cols], preferred_element_type=F32)
                + jnp.dot(inv_hi[...], ylo[:, cols], preferred_element_type=F32)
            )

        edge_time = inverse(slice(extra, extra + LANES))
        for m in range(blocks):
            response = inverse(slice(m * LANES, (m + 1) * LANES))
            rsend[half, m * FFT_BLOCK : (m + 1) * FFT_BLOCK, :] = jnp.where(
                split[m] & (at_block[m] > 0.5), edge_time, response
            ).astype(BF16)
        for j in range(1, shards):
            z_copy(2, half, j).start()
        rbuf[half, :, lane_tile(me_seq)] = rsend[half, my_rows(), :]

    for half in range(halves):
        for j in range(1, groups):
            dp_copy(1, half, j).wait_recv()
    for half in range(halves):
        for j in range(1, shards):
            z_copy(2, half, j).wait_recv()

        @pl.loop(0, shards)
        def _(tile):
            queries = jnp.dot(recv_pick, recv[1, half, :, lane_tile(tile)], preferred_element_type=F32)
            out_ref[:, lane_tile(tile * halves + half)] = (
                queries * rbuf[half, :, lane_tile(tile)].astype(F32)
            ).astype(BF16)

    for half in range(halves):
        for kind in range(2):
            for j in range(1, groups):
                dp_copy(kind, half, j).wait_send()
        for kind in range(3):
            for j in range(1, shards):
                z_copy(kind, half, j).wait_send()


def body(q_arrive, k_arrive, v_arrive, source_rank, first_length, filter_taps):
    groups = lax.axis_size("dp")
    shards = lax.axis_size("seq")
    tokens = q_arrive.shape[1]
    channels = q_arrive.shape[2]
    blocks_here = source_rank.shape[1]
    block_len = tokens // blocks_here
    capacity = max(2, 2 * blocks_here // groups)
    rows = capacity * block_len
    halves = channels // shards // LANES
    blocks = shards * tokens // FFT_BLOCK
    ranks = jnp.repeat(source_rank, block_len, axis=1)
    ranks = jnp.pad(ranks, ((0, -groups % 8), (0, 0)), constant_values=-1)
    tables = [jnp.asarray(table) for table in fourier_tables()]
    vmem = pl.BlockSpec(memory_space=pltpu.VMEM)
    smem = pl.BlockSpec(memory_space=pltpu.SMEM)
    result = pl.pallas_call(
        functools.partial(kernel, groups, shards, halves, rows, block_len),
        out_shape=jax.ShapeDtypeStruct((tokens, channels), BF16),
        in_specs=[vmem, smem] + [vmem] * 8,
        out_specs=vmem,
        scratch_shapes=[
            pltpu.VMEM((2, halves, groups * rows, shards * LANES), BF16),
            pltpu.VMEM((2, halves, groups * rows, shards * LANES), BF16),
            pltpu.VMEM((halves, tokens, shards * LANES), BF16),
            pltpu.VMEM((halves, shards * tokens, LANES), BF16),
            pltpu.VMEM((halves, shards * tokens, LANES), BF16),
            pltpu.VMEM((halves, shards * tokens, LANES), BF16),
            pltpu.VMEM((halves, tokens, shards * LANES), BF16),
            pltpu.VMEM((FFT_BLOCK, (blocks + 1) * LANES), BF16),
            pltpu.VMEM((2 * FFT_BLOCK, (blocks + 1) * LANES), F32),
            pltpu.VMEM((halves, 2 * FFT_BLOCK, blocks * LANES), F32),
            pltpu.VMEM((2 * FFT_BLOCK, (blocks + 1) * LANES), BF16),
            pltpu.VMEM((2 * FFT_BLOCK, (blocks + 1) * LANES), BF16),
            pltpu.SemaphoreType.DMA((2, halves, groups)),
            pltpu.SemaphoreType.DMA((2, halves, groups)),
            pltpu.SemaphoreType.DMA((3, halves, shards)),
            pltpu.SemaphoreType.DMA((3, halves, shards)),
        ],
        compiler_params=pltpu.CompilerParams(
            collective_id=0, has_side_effects=True, vmem_limit_bytes=48 * 1024 * 1024
        ),
    )(ranks, first_length, q_arrive[0], k_arrive[0], v_arrive[0], filter_taps, *tables)
    return result[None]


def solution(mesh):
    return jax.shard_map(
        body,
        mesh=mesh,
        in_specs=(
            P("dp", "seq", None),
            P("dp", "seq", None),
            P("dp", "seq", None),
            P(None, "seq"),
            P(),
            P("seq", None),
        ),
        out_specs=P("dp", "seq", None),
        check_vma=False,
    )
```

```python
import functools
import math

import jax
import jax.numpy as jnp
import ml_dtypes
import numpy as np
from jax import lax
from jax.experimental import pallas as pl
from jax.experimental.pallas import tpu as pltpu
from jax.sharding import PartitionSpec as P

LANES = 128
FFT_BLOCK = 256
FILTER_PARTS = 4
MESH = pl.DeviceIdType.MESH
F32 = jnp.float32
BF16 = jnp.bfloat16


def split_table(table):
    high = table.astype(ml_dtypes.bfloat16)
    low = (table - high.astype(np.float64)).astype(ml_dtypes.bfloat16)
    return high, low


def fourier_tables():
    size = FFT_BLOCK
    freq = np.arange(size)[:, None] * 2 + 1
    angle = math.pi / (2 * size) * (freq * np.arange(size)[None, :] % (4 * size))
    forward = np.concatenate([np.cos(angle), -np.sin(angle)], axis=0)
    places = np.arange(size, 2 * size)[:, None]
    back_angle = math.pi / (2 * size) * (places * freq[:, 0][None, :] % (4 * size))
    inverse = np.concatenate([np.cos(back_angle), -np.sin(back_angle)], axis=1) / size
    return split_table(forward) + split_table(inverse)


def kernel(
    groups, shards, halves, rows, block_len,
    rank_ref, first_ref, q_hbm, k_hbm, v_hbm, f_hbm, fwd_hi_hbm, fwd_lo_hbm, inv_hi_hbm, inv_lo_hbm,
    out_ref,
    q_ref, k_ref, v_ref, f_ref, fwd_hi, fwd_lo, inv_hi, inv_lo,
    packed, recv, xsend, xbuf, fbuf, rsend, rbuf, qbuf, xs, spec, fspec, yhi, ylo,
    load_sem, dp_send, dp_recv, f_send, f_recv, z_send, z_recv,
):
    tokens = q_ref.shape[0]
    part_rows = tokens // FILTER_PARTS
    blocks = shards * tokens // FFT_BLOCK
    width = halves * LANES
    me_dp = lax.axis_index("dp")
    me_seq = lax.axis_index("seq")
    boundary = first_ref[me_dp]

    barrier = pltpu.get_barrier_semaphore()
    for j in range(1, groups):
        pl.semaphore_signal(
            barrier, inc=1, device_id={"dp": lax.rem(me_dp + j, groups)}, device_id_type=MESH
        )
    for j in range(1, shards):
        pl.semaphore_signal(
            barrier, inc=1, device_id={"seq": lax.rem(me_seq + j, shards)}, device_id_type=MESH
        )

    loads = [
        pltpu.make_async_copy(src, dst, load_sem.at[n])
        for n, (src, dst) in enumerate(
            [
                (k_hbm, k_ref),
                (v_hbm, v_ref),
                (f_hbm, f_ref),
                (q_hbm, q_ref),
                (fwd_hi_hbm, fwd_hi),
                (fwd_lo_hbm, fwd_lo),
                (inv_hi_hbm, inv_hi),
                (inv_lo_hbm, inv_lo),
            ]
        )
    ]
    for load in loads:
        load.start()

    def lane_tile(index):
        return pl.ds(pl.multiple_of(index * LANES, LANES), LANES)

    def dp_copy(kind, half, j):
        peer = lax.rem(me_dp + j, groups)
        return pltpu.make_async_remote_copy(
            src_ref=packed.at[kind, half, pl.ds(pl.multiple_of(peer * rows, rows), rows)],
            dst_ref=recv.at[kind, half, pl.ds(pl.multiple_of(me_dp * rows, rows), rows)],
            send_sem=dp_send.at[kind, half, j],
            recv_sem=dp_recv.at[kind, half, j],
            device_id={"dp": peer},
            device_id_type=MESH,
        )

    my_part = lax.rem(me_dp, FILTER_PARTS)

    def part_slice(index):
        return pl.ds(pl.multiple_of(index * part_rows, part_rows), part_rows)

    def f_copy(half, j):
        peer = me_dp - my_part + lax.rem(my_part + j, FILTER_PARTS)
        return pltpu.make_async_remote_copy(
            src_ref=fbuf.at[half, my_part],
            dst_ref=fbuf.at[half, my_part],
            send_sem=f_send.at[half, j],
            recv_sem=f_recv.at[half, j],
            device_id={"dp": peer},
            device_id_type=MESH,
        )

    def my_rows():
        return pl.ds(pl.multiple_of(me_seq * tokens, tokens), tokens)

    def z_copy(kind, half, j):
        peer = lax.rem(me_seq + j, shards)
        if kind == 0:
            src = f_ref.at[part_slice(my_part), lane_tile(peer * halves + half)]
            dst = fbuf.at[half, my_part, part_slice(me_seq)]
        elif kind == 1:
            src = xsend.at[half, :, lane_tile(peer)]
            dst = xbuf.at[half, my_rows()]
        else:
            src = rsend.at[half, pl.ds(pl.multiple_of(peer * tokens, tokens), tokens)]
            dst = rbuf.at[half, :, lane_tile(me_seq)]
        return pltpu.make_async_remote_copy(
            src_ref=src,
            dst_ref=dst,
            send_sem=z_send.at[kind, half, j],
            recv_sem=z_recv.at[kind, half, j],
            device_id={"seq": peer},
            device_id_type=MESH,
        )

    ranks = rank_ref[...]
    own_rank = rank_ref[pl.ds(me_dp, 1), :]
    own_rank = jnp.broadcast_to(own_rank, ranks.shape)
    group_ids = lax.broadcasted_iota(jnp.int32, ranks.shape, 0)
    earlier_row = lax.broadcasted_iota(jnp.int32, (tokens, tokens), 0)
    earlier_col = lax.broadcasted_iota(jnp.int32, (tokens, tokens), 1)
    earlier = jnp.where(
        (earlier_row // block_len < earlier_col // block_len) & (earlier_row % block_len == 0), 1.0, 0.0
    ).astype(BF16)
    inner = (lax.broadcasted_iota(jnp.int32, ranks.shape, 1) % block_len).astype(F32)
    row_ids = lax.broadcasted_iota(jnp.int32, (rows, tokens), 0).astype(F32)

    def one_hot(mask):
        flags = jnp.where(mask, 1.0, 0.0)
        slots = jnp.dot(flags.astype(BF16), earlier, preferred_element_type=F32)
        target = jnp.where(mask, slots * block_len + inner, -1.0)
        return jnp.concatenate(
            [jnp.where(row_ids == target[p : p + 1], 1.0, 0.0) for p in range(groups)], axis=0
        )

    send_pick = one_hot(ranks == me_dp).astype(BF16)
    recv_pick = jnp.transpose(one_hot(own_rank == group_ids)).astype(BF16)

    def pack(kind, half, tile, read):
        values = jnp.concatenate([read(tile * 2), read(tile * 2 + 1)], axis=1)
        moved = jnp.dot(send_pick, values, preferred_element_type=F32).astype(BF16)
        where = pl.ds(pl.multiple_of(tile * 2 * LANES, 2 * LANES), 2 * LANES)
        packed[kind, half, :, where] = moved

    pl.semaphore_wait(barrier, groups + shards - 2)
    loads[2].wait()
    for half in range(halves):
        for j in range(1, shards):
            z_copy(0, half, j).start()
    loads[0].wait()
    loads[1].wait()
    for half in range(halves):

        def product(tile):
            cols = lane_tile(tile * halves + half)
            return (k_ref[:, cols].astype(F32) * v_ref[:, cols].astype(F32)).astype(BF16)

        @pl.loop(0, shards // 2)
        def _(tile):
            pack(0, half, tile, product)

        for j in range(1, groups):
            dp_copy(0, half, j).start()

    loads[3].wait()
    for half in range(halves):

        @pl.loop(0, shards // 2)
        def _(tile):
            pack(1, half, tile, lambda t: q_ref[:, lane_tile(t * halves + half)])

    own = pl.ds(pl.multiple_of(me_dp * rows, rows), rows)
    for half in range(halves):
        for kind in range(2):
            recv[kind, half, own, :] = packed[kind, half, own, :]
        fbuf[half, my_part, part_slice(me_seq), :] = f_ref[
            part_slice(my_part), lane_tile(me_seq * halves + half)
        ]
    for half in range(halves):
        for j in range(1, shards):
            z_copy(0, half, j).wait_recv()
        for j in range(1, FILTER_PARTS):
            f_copy(half, j).start()

    for half in range(halves):
        for j in range(1, groups):
            dp_copy(0, half, j).wait_recv()
        xsend[half] = jnp.dot(recv_pick, recv[0, half], preferred_element_type=F32).astype(BF16)
        for j in range(1, shards):
            z_copy(1, half, j).start()
        xbuf[half, my_rows(), :] = xsend[half, :, lane_tile(me_seq)]
    for half in range(halves):
        for j in range(1, groups):
            dp_copy(1, half, j).start()
    for load in loads[4:]:
        load.wait()

    def forward(values):
        return jnp.dot(fwd_hi[...], values, preferred_element_type=F32) + jnp.dot(
            fwd_lo[...], values, preferred_element_type=F32
        )

    for half in range(halves):
        for j in range(1, FILTER_PARTS):
            f_copy(half, j).wait_recv()

        def filter_block(b):
            ranges = range(b * FFT_BLOCK // tokens, (b + 1) * FFT_BLOCK // tokens)
            return jnp.concatenate(
                [
                    fbuf[half, part, r * part_rows : (r + 1) * part_rows, :]
                    for r in ranges
                    for part in range(FILTER_PARTS)
                ],
                axis=0,
            )

        for b in range(0, blocks, 2):
            fspec[half, :, b * LANES : (b + 2) * LANES] = forward(
                jnp.concatenate([filter_block(b), filter_block(b + 1)], axis=1)
            )

    def holds(condition):
        return jnp.where(condition, 1.0, 0.0).astype(F32)

    at_or_after = [holds(FFT_BLOCK * (i + 1) > boundary) for i in range(blocks)]
    before = [1.0 - flag for flag in at_or_after]
    at_block = [
        holds((FFT_BLOCK * i <= boundary) & (FFT_BLOCK * (i + 1) > boundary)) for i in range(blocks)
    ]
    keep = {
        (i, m): jnp.maximum(at_or_after[i], before[m]) for m in range(blocks) for i in range(m)
    }
    place = lax.broadcasted_iota(jnp.int32, (FFT_BLOCK, LANES), 0)
    split = [
        (place + FFT_BLOCK * i < boundary) & (jnp.full(place.shape, FFT_BLOCK * (i + 1)) > boundary)
        for i in range(blocks)
    ]
    extra = blocks * LANES
    step = 16
    sign = jnp.where(lax.broadcasted_iota(jnp.int32, (step, LANES), 0) % 2 == 0, 1.0, -1.0).astype(F32)

    for half in range(halves):
        for j in range(1, shards):
            z_copy(1, half, j).wait_recv()
        early = jnp.zeros((FFT_BLOCK, LANES), F32)
        for i in range(blocks):
            values = xbuf[half, i * FFT_BLOCK : (i + 1) * FFT_BLOCK, :].astype(F32)
            xs[:, i * LANES : (i + 1) * LANES] = jnp.where(split[i], 0.0, values).astype(BF16)
            early = early + jnp.where(split[i], values, 0.0) * at_block[i]
        xs[:, extra : extra + LANES] = early.astype(BF16)
        for start in range(0, (blocks + 1) * LANES, 2 * LANES):
            stop = min(start + 2 * LANES, (blocks + 1) * LANES)
            spec[:, start:stop] = forward(xs[:, start:stop])

        @pl.loop(0, FFT_BLOCK // step)
        def _(chunk):
            re = pl.ds(pl.multiple_of(chunk * step, step), step)
            im = pl.ds(pl.multiple_of(FFT_BLOCK + chunk * step, step), step)

            def read(ref, b):
                return ref[re, b * LANES : (b + 1) * LANES], ref[im, b * LANES : (b + 1) * LANES]

            x = [read(spec, b) for b in range(blocks + 1)]
            taps = []
            last = None
            for b in range(blocks):
                a_re, a_im = read(fspec.at[half], b)
                g_re, g_im = sign * a_im, -(sign * a_re)
                if last is not None:
                    g_re, g_im = g_re + last[0], g_im + last[1]
                taps.append((g_re, g_im))
                last = (a_re, a_im)

            def times(a, b):
                return a[0] * b[0] - a[1] * b[1], a[0] * b[1] + a[1] * b[0]

            def put(b, value):
                for part, where in zip(value, (re, im)):
                    high = part.astype(BF16)
                    yhi[where, b * LANES : (b + 1) * LANES] = high
                    ylo[where, b * LANES : (b + 1) * LANES] = (part - high.astype(F32)).astype(BF16)

            edge = times(taps[0], x[blocks])
            for m in range(blocks):
                total = times(taps[0], x[m])
                for i in range(m):
                    term = times(taps[m - i], x[i])
                    total = tuple(t + keep[i, m] * s for t, s in zip(total, term))
                    edge = tuple(t + at_block[m] * s for t, s in zip(edge, term))
                put(m, total)
            put(blocks, edge)

        def inverse(cols):
            return (
                jnp.dot(inv_hi[...], yhi[:, cols], preferred_element_type=F32)
                + jnp.dot(inv_lo[...], yhi[:, cols], preferred_element_type=F32)
                + jnp.dot(inv_hi[...], ylo[:, cols], preferred_element_type=F32)
            )

        edge_time = inverse(slice(extra, extra + LANES))
        for start in range(0, blocks, 2):
            response = inverse(slice(start * LANES, (start + 2) * LANES))
            for m in (start, start + 1):
                rsend[half, m * FFT_BLOCK : (m + 1) * FFT_BLOCK, :] = jnp.where(
                    split[m] & (at_block[m] > 0.5),
                    edge_time,
                    response[:, (m - start) * LANES : (m - start + 1) * LANES],
                ).astype(BF16)
        for j in range(1, shards):
            z_copy(2, half, j).start()
        rbuf[half, :, lane_tile(me_seq)] = rsend[half, my_rows(), :]

    for half in range(halves):
        for j in range(1, groups):
            dp_copy(1, half, j).wait_recv()
        qbuf[half] = jnp.dot(recv_pick, recv[1, half], preferred_element_type=F32).astype(BF16)
    for half in range(halves):
        for j in range(1, shards):
            z_copy(2, half, j).wait_recv()
        for tile in range(shards):
            cols = slice(tile * LANES, (tile + 1) * LANES)
            first = (tile * halves + half) * LANES
            out_ref[:, first : first + LANES] = (
                qbuf[half, :, cols].astype(F32) * rbuf[half, :, cols].astype(F32)
            ).astype(BF16)

    for half in range(halves):
        for kind in range(2):
            for j in range(1, groups):
                dp_copy(kind, half, j).wait_send()
        for j in range(1, FILTER_PARTS):
            f_copy(half, j).wait_send()
        for kind in range(3):
            for j in range(1, shards):
                z_copy(kind, half, j).wait_send()


def body(q_arrive, k_arrive, v_arrive, source_rank, first_length, filter_taps):
    groups = lax.axis_size("dp")
    shards = lax.axis_size("seq")
    tokens = q_arrive.shape[1]
    channels = q_arrive.shape[2]
    blocks_here = source_rank.shape[1]
    block_len = tokens // blocks_here
    capacity = max(2, 2 * blocks_here // groups)
    rows = capacity * block_len
    halves = channels // shards // LANES
    blocks = shards * tokens // FFT_BLOCK
    ranks = jnp.repeat(source_rank, block_len, axis=1)
    ranks = jnp.pad(ranks, ((0, -groups % 8), (0, 0)), constant_values=-1)
    tables = [jnp.asarray(table) for table in fourier_tables()]
    vmem = pl.BlockSpec(memory_space=pltpu.VMEM)
    smem = pl.BlockSpec(memory_space=pltpu.SMEM)
    hbm = pl.BlockSpec(memory_space=pltpu.HBM)
    local = pltpu.VMEM((tokens, channels), BF16)
    table_scratch = [pltpu.VMEM(table.shape, BF16) for table in tables]
    result = pl.pallas_call(
        functools.partial(kernel, groups, shards, halves, rows, block_len),
        out_shape=jax.ShapeDtypeStruct((tokens, channels), BF16),
        in_specs=[vmem, smem] + [hbm] * 8,
        out_specs=vmem,
        scratch_shapes=[local] * 4 + table_scratch + [
            pltpu.VMEM((2, halves, groups * rows, shards * LANES), BF16),
            pltpu.VMEM((2, halves, groups * rows, shards * LANES), BF16),
            pltpu.VMEM((halves, tokens, shards * LANES), BF16),
            pltpu.VMEM((halves, shards * tokens, LANES), BF16),
            pltpu.VMEM((halves, FILTER_PARTS, shards * tokens // FILTER_PARTS, LANES), BF16),
            pltpu.VMEM((halves, shards * tokens, LANES), BF16),
            pltpu.VMEM((halves, tokens, shards * LANES), BF16),
            pltpu.VMEM((halves, tokens, shards * LANES), BF16),
            pltpu.VMEM((FFT_BLOCK, (blocks + 1) * LANES), BF16),
            pltpu.VMEM((2 * FFT_BLOCK, (blocks + 1) * LANES), F32),
            pltpu.VMEM((halves, 2 * FFT_BLOCK, blocks * LANES), F32),
            pltpu.VMEM((2 * FFT_BLOCK, (blocks + 1) * LANES), BF16),
            pltpu.VMEM((2 * FFT_BLOCK, (blocks + 1) * LANES), BF16),
            pltpu.SemaphoreType.DMA((8,)),
            pltpu.SemaphoreType.DMA((2, halves, groups)),
            pltpu.SemaphoreType.DMA((2, halves, groups)),
            pltpu.SemaphoreType.DMA((halves, FILTER_PARTS)),
            pltpu.SemaphoreType.DMA((halves, FILTER_PARTS)),
            pltpu.SemaphoreType.DMA((3, halves, shards)),
            pltpu.SemaphoreType.DMA((3, halves, shards)),
        ],
        compiler_params=pltpu.CompilerParams(
            collective_id=0, has_side_effects=True, vmem_limit_bytes=48 * 1024 * 1024
        ),
    )(ranks, first_length, q_arrive[0], k_arrive[0], v_arrive[0], filter_taps, *tables)
    return result[None]


def solution(mesh):
    return jax.shard_map(
        body,
        mesh=mesh,
        in_specs=(
            P("dp", "seq", None),
            P("dp", "seq", None),
            P("dp", "seq", None),
            P(None, "seq"),
            P(),
            P("seq", None),
        ),
        out_specs=P("dp", "seq", None),
        check_vma=False,
    )
```

```python
import functools
import math

import jax
import jax.numpy as jnp
import ml_dtypes
import numpy as np
from jax import lax
from jax.experimental import pallas as pl
from jax.experimental.pallas import tpu as pltpu
from jax.sharding import PartitionSpec as P

LANES = 128
FFT_BLOCK = 256
FILTER_PARTS = 4
MESH = pl.DeviceIdType.MESH
F32 = jnp.float32
BF16 = jnp.bfloat16


def split_table(table):
    high = table.astype(ml_dtypes.bfloat16)
    low = (table - high.astype(np.float64)).astype(ml_dtypes.bfloat16)
    return high, low


def fourier_tables():
    size = FFT_BLOCK
    freq = np.arange(size)[:, None] * 2 + 1
    angle = math.pi / (2 * size) * (freq * np.arange(size)[None, :] % (4 * size))
    forward = np.concatenate([np.cos(angle), -np.sin(angle)], axis=0)
    places = np.arange(size, 2 * size)[:, None]
    back_angle = math.pi / (2 * size) * (places * freq[:, 0][None, :] % (4 * size))
    inverse = np.concatenate([np.cos(back_angle), -np.sin(back_angle)], axis=0) / size
    return np.stack(split_table(forward) + split_table(inverse))


def kernel(
    groups, shards, halves, rows, block_len,
    rank_hbm, first_hbm, q_hbm, k_hbm, v_hbm, f_hbm, tables_hbm,
    out_ref,
    rank_ref, first_ref, q_ref, k_ref, v_ref, f_ref, tables,
    packed, recv, xsend, xbuf, fbuf, rsend, rbuf, qbuf, xs, spec, fspec, yhi, ylo,
    load_sem, dp_send, dp_recv, f_send, f_recv, z_send, z_recv,
):
    tokens = q_ref.shape[0]
    part_rows = tokens // FILTER_PARTS
    blocks = shards * tokens // FFT_BLOCK
    me_dp = lax.axis_index("dp")
    me_seq = lax.axis_index("seq")

    barrier = pltpu.get_barrier_semaphore()
    for j in range(1, groups):
        pl.semaphore_signal(
            barrier, inc=1, device_id={"dp": lax.rem(me_dp + j, groups)}, device_id_type=MESH
        )
    for j in range(1, shards):
        pl.semaphore_signal(
            barrier, inc=1, device_id={"seq": lax.rem(me_seq + j, shards)}, device_id_type=MESH
        )

    loads = [
        pltpu.make_async_copy(src, dst, load_sem.at[n])
        for n, (src, dst) in enumerate(
            [
                (k_hbm, k_ref),
                (v_hbm, v_ref),
                (f_hbm, f_ref),
                (q_hbm, q_ref),
                (tables_hbm, tables),
                (rank_hbm, rank_ref),
                (first_hbm, first_ref),
            ]
        )
    ]
    for load in [loads[5], loads[6], *loads[:5]]:
        load.start()

    def lane_tile(index):
        return pl.ds(pl.multiple_of(index * LANES, LANES), LANES)

    def dp_copy(kind, half, j):
        peer = lax.rem(me_dp + j, groups)
        return pltpu.make_async_remote_copy(
            src_ref=packed.at[kind, half, pl.ds(pl.multiple_of(peer * rows, rows), rows)],
            dst_ref=recv.at[kind, half, pl.ds(pl.multiple_of(me_dp * rows, rows), rows)],
            send_sem=dp_send.at[kind, half, j],
            recv_sem=dp_recv.at[kind, half, j],
            device_id={"dp": peer},
            device_id_type=MESH,
        )

    my_part = lax.rem(me_dp, FILTER_PARTS)

    def part_slice(index):
        return pl.ds(pl.multiple_of(index * part_rows, part_rows), part_rows)

    def f_copy(half, j):
        peer = me_dp - my_part + lax.rem(my_part + j, FILTER_PARTS)
        return pltpu.make_async_remote_copy(
            src_ref=fbuf.at[half, my_part],
            dst_ref=fbuf.at[half, my_part],
            send_sem=f_send.at[half, j],
            recv_sem=f_recv.at[half, j],
            device_id={"dp": peer},
            device_id_type=MESH,
        )

    def my_rows():
        return pl.ds(pl.multiple_of(me_seq * tokens, tokens), tokens)

    def z_copy(kind, half, j):
        peer = lax.rem(me_seq + j, shards)
        if kind == 0:
            src = f_ref.at[part_slice(my_part), lane_tile(peer * halves + half)]
            dst = fbuf.at[half, my_part, part_slice(me_seq)]
        elif kind == 1:
            src = xsend.at[half, :, lane_tile(peer)]
            dst = xbuf.at[half, my_rows()]
        else:
            src = rsend.at[half, pl.ds(pl.multiple_of(peer * tokens, tokens), tokens)]
            dst = rbuf.at[half, :, lane_tile(me_seq)]
        return pltpu.make_async_remote_copy(
            src_ref=src,
            dst_ref=dst,
            send_sem=z_send.at[kind, half, j],
            recv_sem=z_recv.at[kind, half, j],
            device_id={"seq": peer},
            device_id_type=MESH,
        )

    loads[-2].wait()
    widen_row = lax.broadcasted_iota(jnp.int32, (tokens // block_len, tokens), 0)
    widen_col = lax.broadcasted_iota(jnp.int32, (tokens // block_len, tokens), 1)
    widen = jnp.where(widen_col // block_len == widen_row, 1.0, 0.0).astype(BF16)
    ranks = jnp.dot(rank_ref[...].astype(F32).astype(BF16), widen, preferred_element_type=F32)
    group_ids = lax.broadcasted_iota(jnp.int32, ranks.shape, 0)
    own_rank = jnp.sum(jnp.where(group_ids == me_dp, ranks, 0.0), axis=0, keepdims=True)
    own_rank = jnp.broadcast_to(own_rank, ranks.shape)
    earlier_row = lax.broadcasted_iota(jnp.int32, (tokens, tokens), 0)
    earlier_col = lax.broadcasted_iota(jnp.int32, (tokens, tokens), 1)
    earlier = jnp.where(
        (earlier_row // block_len < earlier_col // block_len) & (earlier_row % block_len == 0), 1.0, 0.0
    ).astype(BF16)
    inner = (lax.broadcasted_iota(jnp.int32, ranks.shape, 1) % block_len).astype(F32)
    row_ids = lax.broadcasted_iota(jnp.int32, (rows, tokens), 0).astype(F32)

    def one_hot(mask):
        flags = jnp.where(mask, 1.0, 0.0)
        slots = jnp.dot(flags.astype(BF16), earlier, preferred_element_type=F32)
        target = jnp.where(mask, slots * block_len + inner, -1.0)
        return jnp.concatenate(
            [jnp.where(row_ids == target[p : p + 1], 1.0, 0.0) for p in range(groups)], axis=0
        )

    send_pick = one_hot(ranks == me_dp.astype(F32)).astype(BF16)
    recv_pick = jnp.transpose(one_hot(own_rank == group_ids.astype(F32))).astype(BF16)

    def pack(kind, half, tile, read):
        values = jnp.concatenate([read(tile * 2), read(tile * 2 + 1)], axis=1)
        moved = jnp.dot(send_pick, values, preferred_element_type=F32).astype(BF16)
        where = pl.ds(pl.multiple_of(tile * 2 * LANES, 2 * LANES), 2 * LANES)
        packed[kind, half, :, where] = moved

    pl.semaphore_wait(barrier, groups + shards - 2)
    loads[2].wait()
    for half in range(halves):
        for j in range(1, shards):
            z_copy(0, half, j).start()
    loads[0].wait()
    loads[1].wait()
    for half in range(halves):

        def product(tile):
            cols = lane_tile(tile * halves + half)
            return (k_ref[:, cols].astype(F32) * v_ref[:, cols].astype(F32)).astype(BF16)

        @pl.loop(0, shards // 2)
        def _(tile):
            pack(0, half, tile, product)

        for j in range(1, groups):
            dp_copy(0, half, j).start()

    loads[3].wait()
    for half in range(halves):

        @pl.loop(0, shards // 2)
        def _(tile):
            pack(1, half, tile, lambda t: q_ref[:, lane_tile(t * halves + half)])

    own = pl.ds(pl.multiple_of(me_dp * rows, rows), rows)
    for half in range(halves):
        for kind in range(2):
            recv[kind, half, own, :] = packed[kind, half, own, :]
        fbuf[half, my_part, part_slice(me_seq), :] = f_ref[
            part_slice(my_part), lane_tile(me_seq * halves + half)
        ]
    for half in range(halves):
        for j in range(1, shards):
            z_copy(0, half, j).wait_recv()
        for j in range(1, FILTER_PARTS):
            f_copy(half, j).start()

    for half in range(halves):
        for j in range(1, groups):
            dp_copy(0, half, j).wait_recv()
        xsend[half] = jnp.dot(recv_pick, recv[0, half], preferred_element_type=F32).astype(BF16)
        for j in range(1, shards):
            z_copy(1, half, j).start()
        xbuf[half, my_rows(), :] = xsend[half, :, lane_tile(me_seq)]
    for half in range(halves):
        for j in range(1, groups):
            dp_copy(1, half, j).start()
    for load in [loads[4], loads[6]]:
        load.wait()
    boundary = first_ref[me_dp]

    def forward(values):
        return jnp.dot(tables[0], values, preferred_element_type=F32) + jnp.dot(
            tables[1], values, preferred_element_type=F32
        )

    for half in range(halves):
        for j in range(1, FILTER_PARTS):
            f_copy(half, j).wait_recv()

        def filter_block(b):
            ranges = range(b * FFT_BLOCK // tokens, (b + 1) * FFT_BLOCK // tokens)
            return jnp.concatenate(
                [
                    fbuf[half, part, r * part_rows : (r + 1) * part_rows, :]
                    for r in ranges
                    for part in range(FILTER_PARTS)
                ],
                axis=0,
            )

        for b in range(0, blocks, 2):
            fspec[half, :, b * LANES : (b + 2) * LANES] = forward(
                jnp.concatenate([filter_block(b), filter_block(b + 1)], axis=1)
            )

    def holds(condition):
        return jnp.where(condition, 1.0, 0.0).astype(F32)

    at_or_after = [holds(FFT_BLOCK * (i + 1) > boundary) for i in range(blocks)]
    before = [1.0 - flag for flag in at_or_after]
    at_block = [
        holds((FFT_BLOCK * i <= boundary) & (FFT_BLOCK * (i + 1) > boundary)) for i in range(blocks)
    ]
    keep = {
        (i, m): jnp.maximum(at_or_after[i], before[m]) for m in range(blocks) for i in range(m)
    }
    place = lax.broadcasted_iota(jnp.int32, (FFT_BLOCK, LANES), 0)
    split = [
        (place + FFT_BLOCK * i < boundary) & (jnp.full(place.shape, FFT_BLOCK * (i + 1)) > boundary)
        for i in range(blocks)
    ]
    extra = blocks * LANES
    step = 16
    sign = jnp.where(lax.broadcasted_iota(jnp.int32, (step, LANES), 0) % 2 == 0, 1.0, -1.0).astype(F32)

    for half in range(halves):
        for j in range(1, shards):
            z_copy(1, half, j).wait_recv()
        early = jnp.zeros((FFT_BLOCK, LANES), F32)
        for i in range(blocks):
            values = xbuf[half, i * FFT_BLOCK : (i + 1) * FFT_BLOCK, :].astype(F32)
            xs[:, i * LANES : (i + 1) * LANES] = jnp.where(split[i], 0.0, values).astype(BF16)
            early = early + jnp.where(split[i], values, 0.0) * at_block[i]
        xs[:, extra : extra + LANES] = early.astype(BF16)
        for start in range(0, (blocks + 1) * LANES, 2 * LANES):
            stop = min(start + 2 * LANES, (blocks + 1) * LANES)
            spec[:, start:stop] = forward(xs[:, start:stop])

        @pl.loop(0, FFT_BLOCK // step)
        def _(chunk):
            re = pl.ds(pl.multiple_of(chunk * step, step), step)
            im = pl.ds(pl.multiple_of(FFT_BLOCK + chunk * step, step), step)

            def read(ref, b):
                return ref[re, b * LANES : (b + 1) * LANES], ref[im, b * LANES : (b + 1) * LANES]

            x = [read(spec, b) for b in range(blocks + 1)]
            taps = []
            last = None
            for b in range(blocks):
                a_re, a_im = read(fspec.at[half], b)
                g_re, g_im = sign * a_im, -(sign * a_re)
                if last is not None:
                    g_re, g_im = g_re + last[0], g_im + last[1]
                taps.append((g_re, g_im))
                last = (a_re, a_im)

            def times(a, b):
                return a[0] * b[0] - a[1] * b[1], a[0] * b[1] + a[1] * b[0]

            def put(b, value):
                for part, where in zip(value, (re, im)):
                    high = part.astype(BF16)
                    yhi[where, b * LANES : (b + 1) * LANES] = high
                    ylo[where, b * LANES : (b + 1) * LANES] = (part - high.astype(F32)).astype(BF16)

            edge = times(taps[0], x[blocks])
            for m in range(blocks):
                total = times(taps[0], x[m])
                for i in range(m):
                    term = times(taps[m - i], x[i])
                    total = tuple(t + keep[i, m] * s for t, s in zip(total, term))
                    edge = tuple(t + at_block[m] * s for t, s in zip(edge, term))
                put(m, total)
            put(blocks, edge)

        def back(table, values):
            return jnp.dot(table[:FFT_BLOCK], values[:FFT_BLOCK], preferred_element_type=F32) + jnp.dot(
                table[FFT_BLOCK:], values[FFT_BLOCK:], preferred_element_type=F32
            )

        def inverse(cols):
            return (
                back(tables[2], yhi[:, cols])
                + back(tables[3], yhi[:, cols])
                + back(tables[2], ylo[:, cols])
            )

        edge_time = inverse(slice(extra, extra + LANES))
        for start in range(0, blocks, 2):
            response = inverse(slice(start * LANES, (start + 2) * LANES))
            for m in (start, start + 1):
                rsend[half, m * FFT_BLOCK : (m + 1) * FFT_BLOCK, :] = jnp.where(
                    split[m] & (at_block[m] > 0.5),
                    edge_time,
                    response[:, (m - start) * LANES : (m - start + 1) * LANES],
                ).astype(BF16)
        for j in range(1, shards):
            z_copy(2, half, j).start()
        rbuf[half, :, lane_tile(me_seq)] = rsend[half, my_rows(), :]

    for half in range(halves):
        for j in range(1, groups):
            dp_copy(1, half, j).wait_recv()
        qbuf[half] = jnp.dot(recv_pick, recv[1, half], preferred_element_type=F32).astype(BF16)
    for half in range(halves):
        for j in range(1, shards):
            z_copy(2, half, j).wait_recv()
        for tile in range(shards):
            cols = slice(tile * LANES, (tile + 1) * LANES)
            first = (tile * halves + half) * LANES
            out_ref[:, first : first + LANES] = (
                qbuf[half, :, cols].astype(F32) * rbuf[half, :, cols].astype(F32)
            ).astype(BF16)

    for half in range(halves):
        for kind in range(2):
            for j in range(1, groups):
                dp_copy(kind, half, j).wait_send()
        for j in range(1, FILTER_PARTS):
            f_copy(half, j).wait_send()
        for kind in range(3):
            for j in range(1, shards):
                z_copy(kind, half, j).wait_send()


def body(q_arrive, k_arrive, v_arrive, source_rank, first_length, filter_taps):
    groups = lax.axis_size("dp")
    shards = lax.axis_size("seq")
    tokens = q_arrive.shape[1]
    channels = q_arrive.shape[2]
    blocks_here = source_rank.shape[1]
    block_len = tokens // blocks_here
    capacity = max(2, 2 * blocks_here // groups)
    rows = capacity * block_len
    halves = channels // shards // LANES
    blocks = shards * tokens // FFT_BLOCK
    tables = jnp.asarray(fourier_tables())
    vmem = pl.BlockSpec(memory_space=pltpu.VMEM)
    hbm = pl.BlockSpec(memory_space=pltpu.HBM)
    local = pltpu.VMEM((tokens, channels), BF16)
    result = pl.pallas_call(
        functools.partial(kernel, groups, shards, halves, rows, block_len),
        out_shape=jax.ShapeDtypeStruct((tokens, channels), BF16),
        in_specs=[hbm] * 7,
        out_specs=vmem,
        scratch_shapes=[
            pltpu.VMEM(source_rank.shape, jnp.int32),
            pltpu.SMEM(first_length.shape, jnp.int32),
        ] + [local] * 4 + [pltpu.VMEM(tables.shape, BF16)] + [
            pltpu.VMEM((2, halves, groups * rows, shards * LANES), BF16),
            pltpu.VMEM((2, halves, groups * rows, shards * LANES), BF16),
            pltpu.VMEM((halves, tokens, shards * LANES), BF16),
            pltpu.VMEM((halves, shards * tokens, LANES), BF16),
            pltpu.VMEM((halves, FILTER_PARTS, shards * tokens // FILTER_PARTS, LANES), BF16),
            pltpu.VMEM((halves, shards * tokens, LANES), BF16),
            pltpu.VMEM((halves, tokens, shards * LANES), BF16),
            pltpu.VMEM((halves, tokens, shards * LANES), BF16),
            pltpu.VMEM((FFT_BLOCK, (blocks + 1) * LANES), BF16),
            pltpu.VMEM((2 * FFT_BLOCK, (blocks + 1) * LANES), F32),
            pltpu.VMEM((halves, 2 * FFT_BLOCK, blocks * LANES), F32),
            pltpu.VMEM((2 * FFT_BLOCK, (blocks + 1) * LANES), BF16),
            pltpu.VMEM((2 * FFT_BLOCK, (blocks + 1) * LANES), BF16),
            pltpu.SemaphoreType.DMA((7,)),
            pltpu.SemaphoreType.DMA((2, halves, groups)),
            pltpu.SemaphoreType.DMA((2, halves, groups)),
            pltpu.SemaphoreType.DMA((halves, FILTER_PARTS)),
            pltpu.SemaphoreType.DMA((halves, FILTER_PARTS)),
            pltpu.SemaphoreType.DMA((3, halves, shards)),
            pltpu.SemaphoreType.DMA((3, halves, shards)),
        ],
        compiler_params=pltpu.CompilerParams(
            collective_id=0, has_side_effects=True, vmem_limit_bytes=61500 * 1024
        ),
    )(source_rank, first_length, q_arrive[0], k_arrive[0], v_arrive[0], filter_taps, tables)
    return result[None]


def solution(mesh):
    return jax.shard_map(
        body,
        mesh=mesh,
        in_specs=(
            P("dp", "seq", None),
            P("dp", "seq", None),
            P("dp", "seq", None),
            P(None, "seq"),
            P(),
            P("seq", None),
        ),
        out_specs=P("dp", "seq", None),
        check_vma=False,
    )
```

```python
import functools
import math

import jax
import jax.numpy as jnp
import ml_dtypes
import numpy as np
from jax import lax
from jax.experimental import pallas as pl
from jax.experimental.pallas import tpu as pltpu
from jax.sharding import PartitionSpec as P

LANES = 128
FFT_BLOCK = 256
FILTER_PARTS = 4
MESH = pl.DeviceIdType.MESH
F32 = jnp.float32
BF16 = jnp.bfloat16


def split_table(table):
    high = table.astype(ml_dtypes.bfloat16)
    low = (table - high.astype(np.float64)).astype(ml_dtypes.bfloat16)
    return high, low


def fourier_tables():
    size = FFT_BLOCK
    freq = np.arange(size)[:, None] * 2 + 1
    angle = math.pi / (2 * size) * (freq * np.arange(size)[None, :] % (4 * size))
    forward = np.concatenate([np.cos(angle), -np.sin(angle)], axis=0)
    places = np.arange(size, 2 * size)[:, None]
    back_angle = math.pi / (2 * size) * (places * freq[:, 0][None, :] % (4 * size))
    inverse = np.concatenate([np.cos(back_angle), -np.sin(back_angle)], axis=0) / size
    return np.stack(split_table(forward) + split_table(inverse))


def kernel(
    groups, shards, halves, rows, block_len,
    rank_hbm, first_hbm, q_hbm, k_hbm, v_hbm, f_hbm, tables_hbm,
    out_ref,
    rank_ref, first_ref, q_ref, k_ref, v_ref, f_ref, tables,
    packed, recv, xsend, xbuf, fbuf, rsend, rbuf, qbuf, xs, spec, fspec, yhi, ylo,
    load_sem, dp_send, dp_recv, f_send, f_recv, z_send, z_recv,
):
    tokens = q_ref.shape[0]
    part_rows = tokens // FILTER_PARTS
    blocks = shards * tokens // FFT_BLOCK
    me_dp = lax.axis_index("dp")
    me_seq = lax.axis_index("seq")

    barrier = pltpu.get_barrier_semaphore()
    for j in range(1, groups):
        pl.semaphore_signal(
            barrier, inc=1, device_id={"dp": lax.rem(me_dp + j, groups)}, device_id_type=MESH
        )
    for j in range(1, shards):
        pl.semaphore_signal(
            barrier, inc=1, device_id={"seq": lax.rem(me_seq + j, shards)}, device_id_type=MESH
        )

    loads = [
        pltpu.make_async_copy(src, dst, load_sem.at[n])
        for n, (src, dst) in enumerate(
            [
                (k_hbm, k_ref),
                (v_hbm, v_ref),
                (f_hbm, f_ref),
                (q_hbm, q_ref),
                (tables_hbm, tables),
                (rank_hbm, rank_ref),
                (first_hbm, first_ref),
            ]
        )
    ]
    for load in [loads[5], loads[6], *loads[:5]]:
        load.start()

    def lane_tile(index):
        return pl.ds(pl.multiple_of(index * LANES, LANES), LANES)

    def dp_copy(kind, half, j):
        peer = lax.rem(me_dp + j, groups)
        return pltpu.make_async_remote_copy(
            src_ref=packed.at[kind, half, pl.ds(pl.multiple_of(peer * rows, rows), rows)],
            dst_ref=recv.at[kind, half, pl.ds(pl.multiple_of(me_dp * rows, rows), rows)],
            send_sem=dp_send.at[kind, half, j],
            recv_sem=dp_recv.at[kind, half, j],
            device_id={"dp": peer},
            device_id_type=MESH,
        )

    my_part = lax.rem(me_dp, FILTER_PARTS)

    def part_slice(index):
        return pl.ds(pl.multiple_of(index * part_rows, part_rows), part_rows)

    def f_copy(half, j):
        peer = me_dp - my_part + lax.rem(my_part + j, FILTER_PARTS)
        return pltpu.make_async_remote_copy(
            src_ref=fbuf.at[half, my_part],
            dst_ref=fbuf.at[half, my_part],
            send_sem=f_send.at[half, j],
            recv_sem=f_recv.at[half, j],
            device_id={"dp": peer},
            device_id_type=MESH,
        )

    def my_rows():
        return pl.ds(pl.multiple_of(me_seq * tokens, tokens), tokens)

    def z_copy(kind, half, j):
        peer = lax.rem(me_seq + j, shards)
        if kind == 0:
            src = f_ref.at[part_slice(my_part), lane_tile(peer * halves + half)]
            dst = fbuf.at[half, my_part, part_slice(me_seq)]
        elif kind == 1:
            src = xsend.at[half, :, lane_tile(peer)]
            dst = xbuf.at[half, my_rows()]
        else:
            src = rsend.at[half, pl.ds(pl.multiple_of(peer * tokens, tokens), tokens)]
            dst = rbuf.at[half, :, lane_tile(me_seq)]
        return pltpu.make_async_remote_copy(
            src_ref=src,
            dst_ref=dst,
            send_sem=z_send.at[kind, half, j],
            recv_sem=z_recv.at[kind, half, j],
            device_id={"seq": peer},
            device_id_type=MESH,
        )

    loads[-2].wait()
    widen_row = lax.broadcasted_iota(jnp.int32, (tokens // block_len, tokens), 0)
    widen_col = lax.broadcasted_iota(jnp.int32, (tokens // block_len, tokens), 1)
    widen = jnp.where(widen_col // block_len == widen_row, 1.0, 0.0).astype(BF16)
    ranks = jnp.dot(rank_ref[...].astype(F32).astype(BF16), widen, preferred_element_type=F32)
    group_ids = lax.broadcasted_iota(jnp.int32, ranks.shape, 0)
    own_rank = jnp.sum(jnp.where(group_ids == me_dp, ranks, 0.0), axis=0, keepdims=True)
    own_rank = jnp.broadcast_to(own_rank, ranks.shape)
    earlier_row = lax.broadcasted_iota(jnp.int32, (tokens, tokens), 0)
    earlier_col = lax.broadcasted_iota(jnp.int32, (tokens, tokens), 1)
    earlier = jnp.where(
        (earlier_row // block_len < earlier_col // block_len) & (earlier_row % block_len == 0), 1.0, 0.0
    ).astype(BF16)
    inner = (lax.broadcasted_iota(jnp.int32, ranks.shape, 1) % block_len).astype(F32)
    row_ids = lax.broadcasted_iota(jnp.int32, (rows, tokens), 0).astype(F32)

    def one_hot(mask):
        flags = jnp.where(mask, 1.0, 0.0)
        slots = jnp.dot(flags.astype(BF16), earlier, preferred_element_type=F32)
        target = jnp.where(mask, slots * block_len + inner, -1.0)
        return jnp.concatenate(
            [jnp.where(row_ids == target[p : p + 1], 1.0, 0.0) for p in range(groups)], axis=0
        )

    send_pick = one_hot(ranks == me_dp.astype(F32)).astype(BF16)
    recv_pick = jnp.transpose(one_hot(own_rank == group_ids.astype(F32))).astype(BF16)

    def pack(kind, half, tile, read):
        values = jnp.concatenate([read(tile * 2), read(tile * 2 + 1)], axis=1)
        moved = jnp.dot(send_pick, values, preferred_element_type=F32).astype(BF16)
        where = pl.ds(pl.multiple_of(tile * 2 * LANES, 2 * LANES), 2 * LANES)
        packed[kind, half, :, where] = moved

    pl.semaphore_wait(barrier, groups + shards - 2)
    loads[2].wait()
    for half in range(halves):
        for j in range(1, shards):
            z_copy(0, half, j).start()
    loads[0].wait()
    loads[1].wait()
    for half in range(halves):

        def product(tile):
            cols = lane_tile(tile * halves + half)
            return (k_ref[:, cols].astype(F32) * v_ref[:, cols].astype(F32)).astype(BF16)

        @pl.loop(0, shards // 2, unroll=True)
        def _(tile):
            pack(0, half, tile, product)

        for j in range(1, groups):
            dp_copy(0, half, j).start()

    loads[3].wait()
    for half in range(halves):

        @pl.loop(0, shards // 2, unroll=True)
        def _(tile):
            pack(1, half, tile, lambda t: q_ref[:, lane_tile(t * halves + half)])

    own = pl.ds(pl.multiple_of(me_dp * rows, rows), rows)
    for half in range(halves):
        for kind in range(2):
            recv[kind, half, own, :] = packed[kind, half, own, :]
        fbuf[half, my_part, part_slice(me_seq), :] = f_ref[
            part_slice(my_part), lane_tile(me_seq * halves + half)
        ]
    for half in range(halves):
        for j in range(1, shards):
            z_copy(0, half, j).wait_recv()
        for j in range(1, FILTER_PARTS):
            f_copy(half, j).start()

    for half in range(halves):
        for j in range(1, groups):
            dp_copy(0, half, j).wait_recv()
        for j in range(1, groups):
            dp_copy(1, half, j).start()
        xsend[half] = jnp.dot(recv_pick, recv[0, half], preferred_element_type=F32).astype(BF16)
        for j in range(1, shards):
            z_copy(1, half, j).start()
        xbuf[half, my_rows(), :] = xsend[half, :, lane_tile(me_seq)]
    for load in [loads[4], loads[6]]:
        load.wait()
    boundary = first_ref[me_dp]

    def forward(values):
        return jnp.dot(tables[0], values, preferred_element_type=F32) + jnp.dot(
            tables[1], values, preferred_element_type=F32
        )

    for half in range(halves):
        for j in range(1, FILTER_PARTS):
            f_copy(half, j).wait_recv()

        def filter_block(b):
            ranges = range(b * FFT_BLOCK // tokens, (b + 1) * FFT_BLOCK // tokens)
            return jnp.concatenate(
                [
                    fbuf[half, part, r * part_rows : (r + 1) * part_rows, :]
                    for r in ranges
                    for part in range(FILTER_PARTS)
                ],
                axis=0,
            )

        for b in range(0, blocks, 2):
            fspec[half, :, b * LANES : (b + 2) * LANES] = forward(
                jnp.concatenate([filter_block(b), filter_block(b + 1)], axis=1)
            )

    def holds(condition):
        return jnp.where(condition, 1.0, 0.0).astype(F32)

    at_or_after = [holds(FFT_BLOCK * (i + 1) > boundary) for i in range(blocks)]
    before = [1.0 - flag for flag in at_or_after]
    at_block = [
        holds((FFT_BLOCK * i <= boundary) & (FFT_BLOCK * (i + 1) > boundary)) for i in range(blocks)
    ]
    keep = {
        (i, m): jnp.maximum(at_or_after[i], before[m]) for m in range(blocks) for i in range(m)
    }
    place = lax.broadcasted_iota(jnp.int32, (FFT_BLOCK, LANES), 0)
    split = [
        (place + FFT_BLOCK * i < boundary) & (jnp.full(place.shape, FFT_BLOCK * (i + 1)) > boundary)
        for i in range(blocks)
    ]
    extra = blocks * LANES
    step = 16
    sign = jnp.where(lax.broadcasted_iota(jnp.int32, (step, LANES), 0) % 2 == 0, 1.0, -1.0).astype(F32)

    for half in range(halves):
        for j in range(1, shards):
            z_copy(1, half, j).wait_recv()
        early = jnp.zeros((FFT_BLOCK, LANES), F32)
        for i in range(blocks):
            values = xbuf[half, i * FFT_BLOCK : (i + 1) * FFT_BLOCK, :].astype(F32)
            xs[:, i * LANES : (i + 1) * LANES] = jnp.where(split[i], 0.0, values).astype(BF16)
            early = early + jnp.where(split[i], values, 0.0) * at_block[i]
        xs[:, extra : extra + LANES] = early.astype(BF16)
        for start in range(0, (blocks + 1) * LANES, 2 * LANES):
            stop = min(start + 2 * LANES, (blocks + 1) * LANES)
            spec[:, start:stop] = forward(xs[:, start:stop])

        @pl.loop(0, FFT_BLOCK // step)
        def _(chunk):
            re = pl.ds(pl.multiple_of(chunk * step, step), step)
            im = pl.ds(pl.multiple_of(FFT_BLOCK + chunk * step, step), step)

            def read(ref, b):
                return ref[re, b * LANES : (b + 1) * LANES], ref[im, b * LANES : (b + 1) * LANES]

            x = [read(spec, b) for b in range(blocks + 1)]
            taps = []
            last = None
            for b in range(blocks):
                a_re, a_im = read(fspec.at[half], b)
                g_re, g_im = sign * a_im, -(sign * a_re)
                if last is not None:
                    g_re, g_im = g_re + last[0], g_im + last[1]
                taps.append((g_re, g_im))
                last = (a_re, a_im)

            def times(a, b):
                return a[0] * b[0] - a[1] * b[1], a[0] * b[1] + a[1] * b[0]

            def put(b, value):
                for part, where in zip(value, (re, im)):
                    high = part.astype(BF16)
                    yhi[where, b * LANES : (b + 1) * LANES] = high
                    ylo[where, b * LANES : (b + 1) * LANES] = (part - high.astype(F32)).astype(BF16)

            edge = times(taps[0], x[blocks])
            for m in range(blocks):
                total = times(taps[0], x[m])
                for i in range(m):
                    term = times(taps[m - i], x[i])
                    total = tuple(t + keep[i, m] * s for t, s in zip(total, term))
                    edge = tuple(t + at_block[m] * s for t, s in zip(edge, term))
                put(m, total)
            put(blocks, edge)

        def back(table, values):
            return jnp.dot(table[:FFT_BLOCK], values[:FFT_BLOCK], preferred_element_type=F32) + jnp.dot(
                table[FFT_BLOCK:], values[FFT_BLOCK:], preferred_element_type=F32
            )

        def inverse(cols):
            return (
                back(tables[2], yhi[:, cols])
                + back(tables[3], yhi[:, cols])
                + back(tables[2], ylo[:, cols])
            )

        edge_time = inverse(slice(extra, extra + LANES))
        for start in range(0, blocks, 2):
            response = inverse(slice(start * LANES, (start + 2) * LANES))
            for m in (start, start + 1):
                rsend[half, m * FFT_BLOCK : (m + 1) * FFT_BLOCK, :] = jnp.where(
                    split[m] & (at_block[m] > 0.5),
                    edge_time,
                    response[:, (m - start) * LANES : (m - start + 1) * LANES],
                ).astype(BF16)
        for j in range(1, shards):
            z_copy(2, half, j).start()
        rbuf[half, :, lane_tile(me_seq)] = rsend[half, my_rows(), :]

    for half in range(halves):
        for j in range(1, groups):
            dp_copy(1, half, j).wait_recv()
        qbuf[half] = jnp.dot(recv_pick, recv[1, half], preferred_element_type=F32).astype(BF16)
    for half in range(halves):
        for j in range(1, shards):
            z_copy(2, half, j).wait_recv()
        for tile in range(shards):
            cols = slice(tile * LANES, (tile + 1) * LANES)
            first = (tile * halves + half) * LANES
            out_ref[:, first : first + LANES] = (
                qbuf[half, :, cols].astype(F32) * rbuf[half, :, cols].astype(F32)
            ).astype(BF16)

    for half in range(halves):
        for kind in range(2):
            for j in range(1, groups):
                dp_copy(kind, half, j).wait_send()
        for j in range(1, FILTER_PARTS):
            f_copy(half, j).wait_send()
        for kind in range(3):
            for j in range(1, shards):
                z_copy(kind, half, j).wait_send()


def body(q_arrive, k_arrive, v_arrive, source_rank, first_length, filter_taps):
    groups = lax.axis_size("dp")
    shards = lax.axis_size("seq")
    tokens = q_arrive.shape[1]
    channels = q_arrive.shape[2]
    blocks_here = source_rank.shape[1]
    block_len = tokens // blocks_here
    capacity = max(2, 2 * blocks_here // groups)
    rows = capacity * block_len
    halves = channels // shards // LANES
    blocks = shards * tokens // FFT_BLOCK
    tables = jnp.asarray(fourier_tables())
    vmem = pl.BlockSpec(memory_space=pltpu.VMEM)
    hbm = pl.BlockSpec(memory_space=pltpu.HBM)
    local = pltpu.VMEM((tokens, channels), BF16)
    result = pl.pallas_call(
        functools.partial(kernel, groups, shards, halves, rows, block_len),
        out_shape=jax.ShapeDtypeStruct((tokens, channels), BF16),
        in_specs=[hbm] * 7,
        out_specs=vmem,
        scratch_shapes=[
            pltpu.VMEM(source_rank.shape, jnp.int32),
            pltpu.SMEM(first_length.shape, jnp.int32),
        ] + [local] * 4 + [pltpu.VMEM(tables.shape, BF16)] + [
            pltpu.VMEM((2, halves, groups * rows, shards * LANES), BF16),
            pltpu.VMEM((2, halves, groups * rows, shards * LANES), BF16),
            pltpu.VMEM((halves, tokens, shards * LANES), BF16),
            pltpu.VMEM((halves, shards * tokens, LANES), BF16),
            pltpu.VMEM((halves, FILTER_PARTS, shards * tokens // FILTER_PARTS, LANES), BF16),
            pltpu.VMEM((halves, shards * tokens, LANES), BF16),
            pltpu.VMEM((halves, tokens, shards * LANES), BF16),
            pltpu.VMEM((halves, tokens, shards * LANES), BF16),
            pltpu.VMEM((FFT_BLOCK, (blocks + 1) * LANES), BF16),
            pltpu.VMEM((2 * FFT_BLOCK, (blocks + 1) * LANES), F32),
            pltpu.VMEM((halves, 2 * FFT_BLOCK, blocks * LANES), F32),
            pltpu.VMEM((2 * FFT_BLOCK, (blocks + 1) * LANES), BF16),
            pltpu.VMEM((2 * FFT_BLOCK, (blocks + 1) * LANES), BF16),
            pltpu.SemaphoreType.DMA((7,)),
            pltpu.SemaphoreType.DMA((2, halves, groups)),
            pltpu.SemaphoreType.DMA((2, halves, groups)),
            pltpu.SemaphoreType.DMA((halves, FILTER_PARTS)),
            pltpu.SemaphoreType.DMA((halves, FILTER_PARTS)),
            pltpu.SemaphoreType.DMA((3, halves, shards)),
            pltpu.SemaphoreType.DMA((3, halves, shards)),
        ],
        compiler_params=pltpu.CompilerParams(
            collective_id=0, has_side_effects=True, vmem_limit_bytes=61500 * 1024
        ),
    )(source_rank, first_length, q_arrive[0], k_arrive[0], v_arrive[0], filter_taps, tables)
    return result[None]


def solution(mesh):
    return jax.shard_map(
        body,
        mesh=mesh,
        in_specs=(
            P("dp", "seq", None),
            P("dp", "seq", None),
            P("dp", "seq", None),
            P(None, "seq"),
            P(),
            P("seq", None),
        ),
        out_specs=P("dp", "seq", None),
        check_vma=False,
    )
```
